512 devices in a mesh: ctx: 64 (over y_lo, z, core), head: 8 (over y_hi, x).
Axes of the slice: x: 4, y: 8 (y_hi: 2, y_lo: 4; y = y_hi * 4 + y_lo), z: 8, core: 2. Of those that a mesh axis runs over, the one named last changes fastest.
Arguments:
- queries: bfloat16 [32, 65536, 128], P('head', 'ctx'), may hold values from -8 to 8
- cache_keys: bfloat16 [8, 131072, 128], P('head', 'ctx'), may hold values from -8 to 8
- cache_values: bfloat16 [8, 131072, 128], P('head', 'ctx'), may hold values from -8 to 8
- stretch_keys: bfloat16 [8, 65536, 128], P('head', 'ctx'), may hold values from -8 to 8
- stretch_values: bfloat16 [8, 65536, 128], P('head', 'ctx'), may hold values from -8 to 8
- verticals: int32 [8, 8], P('head'), may hold values from 0 to 1023, as said below
- slashes: int32 [8, 4], P('head'), may hold values from 1 to 32, as said below
Outputs:
- attended: bfloat16 [32, 65536, 128], P('head', 'ctx')
The draws below stay inside these ranges and needn't reach their ends.
Inputs may be any that keep to these rules, and one draw needn't show every extreme that they name: `verticals`: each row names 8 different blocks; block 0 and the last block of the prefix are in every row, and 2 of a row's blocks lie below 16. `slashes`: entry i of a row (i = 1 to 4) lies above (i - 1) * 8 and at most at i * 8; the last entry equals 32.
All inputs are finite; a program needn't handle non-finite values.
Results may differ from the reference program's by a relative error of at most 0.0049.
Values may be sent and summed in bfloat16 or wider, within the bound.
A program may use at most 64 MiB of HBM per device.

```python
import math
import jax
import jax.numpy as jnp
from jax import lax

HEADS = 32
KV_HEADS = 8
HD = 128
BLK = 128
NV = 8
SPAN = 4
QDEV = 1024
CACHE_DEV = 2048
GROUP = 4
STRETCH = 65536
PREFIX = 131072


def draw_queries(key, part):
    key = jax.random.fold_in(key, 3)
    base = jnp.clip(1.5 * jax.random.normal(key, (HEADS, STRETCH, HD), jnp.float32), -7.5, 7.5)
    return base.astype(jnp.bfloat16)


def draw_cache_keys(key, part):
    key = jax.random.fold_in(key, 5)
    base = jnp.clip(1.5 * jax.random.normal(key, (KV_HEADS, PREFIX, HD), jnp.float32), -7.5, 7.5)
    return base.astype(jnp.bfloat16)


def draw_stretch_keys(key, part):
    key = jax.random.fold_in(key, 6)
    base = jnp.clip(1.5 * jax.random.normal(key, (KV_HEADS, STRETCH, HD), jnp.float32), -7.5, 7.5)
    return base.astype(jnp.bfloat16)


def draw_verticals(key, part):
    key = jax.random.fold_in(key, 7)
    device_blocks = CACHE_DEV // BLK
    prefix_blocks = PREFIX // BLK

    def one_row(row_key):
        first_key, other_key = jax.random.split(row_key)
        sink_side = 1 + jax.random.permutation(first_key, device_blocks - 1)[:NV // 4 - 1]
        elsewhere = device_blocks + jax.random.permutation(other_key, prefix_blocks - device_blocks - 1)[:NV - NV // 4 - 1]
        return jnp.concatenate([jnp.zeros((1,), jnp.int32), sink_side.astype(jnp.int32), elsewhere.astype(jnp.int32), jnp.full((1,), prefix_blocks - 1, jnp.int32)])
    return jax.vmap(one_row)(jax.random.split(key, KV_HEADS))


def draw_slashes(key, part):
    key = jax.random.fold_in(key, 9)
    per_device = QDEV // BLK
    lowered = jax.random.randint(key, (KV_HEADS, SPAN), 0, per_device, dtype=jnp.int32)
    last_col = jnp.arange(SPAN, dtype=jnp.int32) == SPAN - 1
    lowered = jnp.where(last_col[None, :], 0, lowered)
    return (jnp.arange(1, SPAN + 1, dtype=jnp.int32) * per_device)[None, :] - lowered


def steps_of(own_key, shape, cuts, low, top_value):
    gain = 1.0
    for axis_at, parts in cuts:
        heights = jax.random.uniform(jax.random.fold_in(jax.random.fold_in(own_key, 6), axis_at), (parts,), jnp.float32, low / len(cuts), top_value / len(cuts))
        gain = gain * jnp.repeat(jnp.exp(heights), shape[axis_at] // parts).reshape((-1,) + (1,) * (len(shape) - 1 - axis_at))
    return gain


def bell_draw(stream_key, shape, scale, limit, pieces=(), held_as=jnp.bfloat16):
    drawn = jax.random.normal(stream_key, shape, jnp.float32) * scale
    if len(pieces) > 0:
        drawn = steps_of(stream_key, shape, pieces, -0.22, 0.18) * drawn
    return jnp.clip(drawn, min=-limit, max=limit).astype(held_as)


def setup_inputs(seed: int = 0) -> dict:
    splits = jax.random.split(jax.random.key(seed), 8)
    queries = draw_queries(jax.random.fold_in(splits[7], 71), 0)
    cache_keys = draw_cache_keys(jax.random.fold_in(splits[7], 71), 0)
    cache_values = bell_draw(splits[2], (KV_HEADS, PREFIX, HD), 2.0, 8.0, ((0, 8), (1, 64)))
    stretch_keys = draw_stretch_keys(jax.random.fold_in(splits[7], 71), 0)
    stretch_values = bell_draw(splits[4], (KV_HEADS, STRETCH, HD), 2.0, 8.0, ((0, 8), (1, 64)))
    verticals = draw_verticals(jax.random.fold_in(splits[7], 71), 0)
    slashes = draw_slashes(jax.random.fold_in(splits[7], 71), 0)
    return {"queries": queries, "cache_keys": cache_keys, "cache_values": cache_values, "stretch_keys": stretch_keys, "stretch_values": stretch_values, "verticals": verticals, "slashes": slashes}


def reference(queries, cache_keys, cache_values, stretch_keys, stretch_values, verticals, slashes):
    stretch_blocks = STRETCH // BLK
    prefix_blocks = PREFIX // BLK
    logit_scale = 1.0 / math.sqrt(HD)
    inside = jnp.arange(BLK, dtype=jnp.int32)
    diagonal_ok = inside[None, :] <= inside[:, None]
    block_ids = jnp.arange(stretch_blocks, dtype=jnp.int32)

    def one_head(head):
        kv_index = head // GROUP
        listed = verticals[kv_index]
        offsets = slashes[kv_index]
        remote_keys = cache_keys[kv_index].reshape(prefix_blocks, BLK, HD)[listed].reshape(NV * BLK, HD).astype(jnp.float32)
        remote_values = cache_values[kv_index].reshape(prefix_blocks, BLK, HD)[listed].reshape(NV * BLK, HD).astype(jnp.float32)
        own_keys = stretch_keys[kv_index].reshape(stretch_blocks, BLK, HD)
        own_values = stretch_values[kv_index].reshape(stretch_blocks, BLK, HD)
        source = block_ids[:, None] - offsets[None, :]
        usable = source >= 0
        source = jnp.maximum(source, 0).astype(jnp.int32)
        local_keys = jnp.concatenate([own_keys[source].reshape(stretch_blocks, SPAN * BLK, HD), own_keys], axis=1).astype(jnp.float32)
        local_values = jnp.concatenate([own_values[source].reshape(stretch_blocks, SPAN * BLK, HD), own_values], axis=1).astype(jnp.float32)
        query_matrix = queries[head].reshape(stretch_blocks, BLK, HD).astype(jnp.float32)
        distant_scores = jnp.einsum('uxt,lt->uxl', query_matrix, remote_keys) * logit_scale
        nearby_scores = jnp.einsum('ohx,ojx->ohj', query_matrix, local_keys) * logit_scale
        band_ok = jnp.broadcast_to(jnp.repeat(usable, BLK, axis=1)[:, None, :], (stretch_blocks, BLK, SPAN * BLK))
        self_ok = jnp.broadcast_to(diagonal_ok[None], (stretch_blocks, BLK, BLK))
        allowed = jnp.concatenate([band_ok, self_ok], axis=2)
        nearby_scores = jnp.where(allowed, nearby_scores, -jnp.inf)
        highest = jnp.maximum(lax.optimization_barrier(jnp.max(distant_scores, axis=-1)), lax.optimization_barrier(jnp.max(nearby_scores, axis=-1)))[..., None]
        distant_exp = jnp.exp(distant_scores - highest)
        nearby_exp = jnp.exp(nearby_scores - highest)
        row_sum = lax.optimization_barrier(jnp.sum(distant_exp, axis=-1, keepdims=True)) + lax.optimization_barrier(jnp.sum(nearby_exp, axis=-1, keepdims=True))
        distant_weight = lax.optimization_barrier((distant_exp / row_sum).astype(jnp.bfloat16)).astype(jnp.float32)
        nearby_weight = lax.optimization_barrier((nearby_exp / row_sum).astype(jnp.bfloat16)).astype(jnp.float32)
        attention_output = jnp.einsum('out,tv->ouv', distant_weight, remote_values) + jnp.einsum('pnt,ptc->pnc', nearby_weight, local_values)
        return attention_output.reshape(STRETCH, HD).astype(jnp.bfloat16)
    return lax.map(one_head, jnp.arange(HEADS, dtype=jnp.int32))
```

```python
import math

import jax
import jax.numpy as jnp
from jax import lax
from jax.experimental import pallas as pl
from jax.experimental.pallas import tpu as pltpu
from jax.sharding import PartitionSpec as P

BLK = 128
HD = 128
NV = 8
SPAN = 4
GROUP = 4
NY, NZ = 4, 8
LAST = 2 * NY * NZ
QROWS = 1024
QB = QROWS // BLK
CROWS = 2048
CB = CROWS // BLK
PART = BLK // NY
QUARTER = NV * PART
MESH = pl.DeviceIdType.MESH
COEF = math.log2(math.e) / math.sqrt(HD)
F32 = jnp.float32
BF16 = jnp.bfloat16


def tile(q, k, v, m, acc, keep=None):
    scores = lax.dot_general(q, k, (((1,), (1,)), ((), ())), preferred_element_type=F32)
    if keep is not None:
        scores = jnp.where(keep, scores, -jnp.inf)
    top = jnp.max(scores, axis=1, keepdims=True)
    new = top if m is None else jnp.maximum(m, top)
    p = jnp.exp2((scores - new) * COEF).astype(BF16)
    o = jnp.dot(p, v, preferred_element_type=F32)
    if m is not None:
        o = acc * jnp.exp2((m - new) * COEF) + o
    return new, o


def kernel(
    verts, slashes, q_hbm, ck_hbm, cv_hbm, sk_hbm, sv_hbm, out_hbm,
    q_v, cache, ring,
    gate, offer, pair, mixed, yb, zb1, zb2, far, far_v,
    near_k, near_v, acc_s, max_s, out_v,
    in_sem, out_sem, pair_sem, y_sem, z1_sem, z2_sem, ag_sem, fs_sem, a1_sem, a2_sem, s1_sem, s2_sem,
):
    me = lax.axis_index("ctx")
    c = lax.rem(me, 2)
    z = lax.rem(me // 2, NZ)
    y = me // (2 * NZ)

    def at(yy, zz, cc):
        return {"ctx": (yy * NZ + zz) * 2 + cc}

    sibling = at(y, z, 1 - c)
    y_peer = [at(lax.rem(y + k, NY), z, c) for k in range(1, NY)]
    z_peer = {k: at(y, lax.rem(z + k + NZ, NZ), c) for k in (-3, -1, 1, 3)}
    ahead = {"ctx": lax.rem(me + 2, LAST)}
    behind = {"ctx": lax.rem(me - 2 + LAST, LAST)}
    a2, s2, a1, s1, own = (ring.at[:, i * QB : (i + 1) * QB] for i in range(SPAN + 1))
    sends = me + 2 < LAST
    gets1 = me >= 2
    gets2 = me >= 4

    loads = [
        pltpu.make_async_copy(ck_hbm, cache.at[0], in_sem.at[0]),
        pltpu.make_async_copy(cv_hbm, cache.at[1], in_sem.at[1]),
        pltpu.make_async_copy(sk_hbm, own.at[0], in_sem.at[2]),
        pltpu.make_async_copy(sv_hbm, own.at[1], in_sem.at[3]),
        pltpu.make_async_copy(q_hbm, q_v, in_sem.at[4]),
    ]
    for load in loads:
        load.start()

    barrier = pltpu.get_barrier_semaphore()
    peers = [sibling] + y_peer + list(z_peer.values()) + [ahead, behind]
    for peer in peers:
        pl.semaphore_signal(barrier, inc=1, device_id=peer, device_id_type=MESH)

    loads[0].wait()
    loads[1].wait()
    for j in range(NV):
        block = lax.rem(verts[0, j], CB)
        mine = cache[pl.ds(c, 1), pl.ds(block, 1)].reshape(NY, PART, HD)
        other = cache[pl.ds(1 - c, 1), pl.ds(block, 1)].reshape(NY, PART, HD)
        pair[pl.ds(c, 1), :, j * PART : (j + 1) * PART, :] = mine[None]
        offer[:, j * PART : (j + 1) * PART, :] = other
    loads[2].wait()
    loads[3].wait()

    pl.semaphore_wait(barrier, len(peers))

    def remote(src, dst, send_sem, recv_sem, to):
        return pltpu.make_async_remote_copy(
            src_ref=src, dst_ref=dst, send_sem=send_sem, recv_sem=recv_sem, device_id=to, device_id_type=MESH
        )

    pair_out = remote(offer, pair.at[c], pair_sem.at[0], pair_sem.at[1], sibling)
    pair_in = remote(offer, pair.at[1 - c], pair_sem.at[0], pair_sem.at[1], sibling)
    pair_out.start()

    def hop(src, dst, sem, kv, to):
        return remote(src.at[kv], dst.at[kv], sem.at[kv], sem.at[2 + kv], to)

    @pl.when(sends)
    def _():
        for kv in (0, 1):
            hop(own, a1, a1_sem, kv, ahead).start()

    @pl.when(c == 0)
    def _():
        for kv in (0, 1):
            hop(own, s1, s1_sem, kv, sibling).start()

    @pl.when(jnp.logical_not(gets1))
    def _():
        ring[:, 2 * QB : 3 * QB] = jnp.zeros((2, QB, BLK, HD), BF16)

    @pl.when(jnp.logical_not(gets2))
    def _():
        ring[:, :QB] = jnp.zeros((2, QB, BLK, HD), BF16)

    gate[0] = jnp.zeros((BLK, HD), BF16)
    gate[1] = jnp.ones((BLK, HD), BF16)
    far_v[:, HD:] = jnp.ones((NY * QUARTER, HD), BF16)

    def owner(j):
        dev = lax.div(verts[0, j], CB)
        return lax.div(dev, 2 * NZ), lax.rem(lax.div(dev, 2), NZ), lax.rem(dev, 2)

    def one_if(lo, hi, x):
        return jnp.minimum(jnp.maximum(x - (lo - 1), 0), 1) * jnp.minimum(jnp.maximum(hi + 1 - x, 0), 1)

    def part(j):
        return slice(j * PART, (j + 1) * PART)

    pair_in.wait_recv()
    for j in range(NV):
        oc = owner(j)[2]
        mixed[:, part(j), :] = pair[pl.ds(oc, 1), :, part(j), :][0]
    y_out = []
    for k in range(1, NY):
        to = lax.rem(y + k, NY)
        y_out.append(remote(mixed.at[to], yb.at[y], y_sem.at[k - 1], y_sem.at[2 + k], y_peer[k - 1]))
        y_out[-1].start()
    yb[pl.ds(y, 1)] = mixed[pl.ds(y, 1)]
    for k in range(1, NY):
        frm = lax.rem(y + NY - k, NY)
        remote(mixed.at[frm], yb.at[frm], y_sem.at[k - 1], y_sem.at[2 + k], y_peer[k - 1]).wait_recv()

    for j in range(NV):
        oy = owner(j)[0]
        zb1[1, part(j), :] = yb[pl.ds(oy, 1), part(j), :][0]
    z1_out = [
        remote(zb1.at[1], zb1.at[0], z1_sem.at[0], z1_sem.at[2], z_peer[1]),
        remote(zb1.at[1], zb1.at[2], z1_sem.at[1], z1_sem.at[3], z_peer[-1]),
    ]
    for copy in z1_out:
        copy.start()
    for copy in z1_out:
        copy.wait_recv()
    for j in range(NV):
        off = lax.rem(owner(j)[1] - z + NZ, NZ)
        slot = 1 + one_if(1, 1, off) - one_if(NZ - 1, NZ - 1, off)
        zb2[1, part(j), :] = zb1[pl.ds(slot, 1), part(j), :][0]
    z2_out = [
        remote(zb2.at[1], zb2.at[0], z2_sem.at[0], z2_sem.at[2], z_peer[3]),
        remote(zb2.at[1], zb2.at[2], z2_sem.at[1], z2_sem.at[3], z_peer[-3]),
    ]
    for copy in z2_out:
        copy.start()

    for kv in (0, 1):

        @pl.when(gets1)
        def _():
            hop(own, a1, a1_sem, kv, behind).wait_recv()

        @pl.when(jnp.logical_and(gets1, sends))
        def _():
            hop(a1, a2, a2_sem, kv, ahead).start()

        @pl.when(c == 0)
        def _():
            hop(a1, s2, s2_sem, kv, sibling).start()

        @pl.when(c == 1)
        def _():
            hop(a1, s1, s1_sem, kv, sibling).start()

    for copy in z2_out:
        copy.wait_recv()
    for j in range(NV):
        off = lax.rem(owner(j)[1] - z + NZ, NZ)
        slot = 1 + one_if(2, 4, off) - one_if(5, 6, off)
        far[pl.ds(c, 1), pl.ds(y, 1), part(j), :] = zb2[pl.ds(slot, 1), part(j), :][None]

    ag_out = []
    for k in range(1, NY):
        ag_out.append(remote(far.at[c, y], far.at[c, y], ag_sem.at[k - 1], ag_sem.at[2 + k], y_peer[k - 1]))
        ag_out[-1].start()
    fs_out = [remote(far.at[c, y], far.at[c, y], fs_sem.at[0], fs_sem.at[NY], sibling)]
    fs_out[0].start()
    for k in range(1, NY):
        frm = lax.rem(y + NY - k, NY)
        remote(far.at[c, frm], far.at[c, frm], ag_sem.at[k - 1], ag_sem.at[2 + k], y_peer[k - 1]).wait_recv()
        fs_out.append(remote(far.at[c, frm], far.at[c, frm], fs_sem.at[k], fs_sem.at[NY + k], sibling))
        fs_out[-1].start()

    for kv in (0, 1):

        @pl.when(gets2)
        def _():
            hop(a1, a2, a2_sem, kv, behind).wait_recv()

        @pl.when(c == 1)
        def _():
            hop(a2, s2, s2_sem, kv, sibling).start()

    for kv in (0, 1):
        hop(own, s1, s1_sem, kv, sibling).wait_recv()
        hop(a1, s2, s2_sem, kv, sibling).wait_recv()

    loads[4].wait()

    def near_block(b, _):
        here = pl.multiple_of(b * BLK, BLK)
        last = SPAN * QB + b
        first = jnp.broadcast_to(ring[0, last, 0:16, :][0:1], (BLK, HD))
        for i in range(SPAN):
            s = slashes[0, i]
            counts = jnp.minimum(jnp.maximum(me * QB + b - s + 1, 0), 1)
            yes = gate[pl.ds(counts, 1)][0]
            no = gate[pl.ds(1 - counts, 1)][0]
            rows = slice(i * BLK, (i + 1) * BLK)
            near_k[b, rows, :] = ring[0, pl.ds(last - s, 1)][0] * yes + first * no
            near_v[b, rows, :HD] = ring[1, pl.ds(last - s, 1)][0] * yes
            near_v[b, rows, HD:] = yes
        rows = slice(SPAN * BLK, (SPAN + 1) * BLK)
        near_k[b, rows, :] = ring[0, last]
        near_v[b, rows, :HD] = ring[1, last]
        near_v[b, rows, HD:] = jnp.ones((BLK, HD), BF16)

        q = q_v[:, pl.ds(here, BLK), :].reshape(GROUP * BLK, HD)
        acc = m = None
        for lo, hi in ((0, 256), (256, 512), (512, 640)):
            keep = None
            if lo == SPAN * BLK:
                t = lax.rem(lax.broadcasted_iota(jnp.int32, (GROUP * BLK, BLK), 0), BLK)
                keep = lax.broadcasted_iota(jnp.int32, (GROUP * BLK, BLK), 1) <= t
            m, acc = tile(q, near_k[b, lo:hi, :], near_v[b, lo:hi, :], m, acc, keep)
        acc_s[:, pl.ds(here, BLK), :] = acc.reshape(GROUP, BLK, 2 * HD)
        max_s[:, pl.ds(here, BLK), :] = jnp.broadcast_to(m, (GROUP * BLK, HD)).reshape(GROUP, BLK, HD)
        return 0

    lax.fori_loop(0, QB, near_block, 0, unroll=True)

    fs_out[0].wait_recv()
    for k in range(1, NY):
        fs_out[k].wait_recv()
    far_v[:, :HD] = far[1].reshape(NY * QUARTER, HD)

    for t in range(NY):

        def far_head(h, _):
            m, acc = jnp.max(max_s[h], axis=1, keepdims=True), acc_s[h]
            m, acc = tile(q_v[h], far[0, t], far_v[t * QUARTER : (t + 1) * QUARTER, :], m, acc)
            if t < NY - 1:
                acc_s[h] = acc
                max_s[h] = jnp.broadcast_to(m, (QROWS, HD))
            else:
                out_v[h] = (acc[:, :HD] / acc[:, HD:]).astype(BF16)
                pltpu.make_async_copy(out_v.at[h], out_hbm.at[h], out_sem.at[h]).start()
            return 0

        lax.fori_loop(0, GROUP, far_head, 0, unroll=True)

    for h in range(GROUP):
        pltpu.make_async_copy(out_v.at[h], out_hbm.at[h], out_sem.at[h]).wait()
    for copy in [pair_out] + y_out + z1_out + z2_out + ag_out + fs_out:
        copy.wait_send()
    for kv in (0, 1):

        @pl.when(sends)
        def _():
            hop(own, a1, a1_sem, kv, ahead).wait_send()

        @pl.when(jnp.logical_and(gets1, sends))
        def _():
            hop(a1, a2, a2_sem, kv, ahead).wait_send()

        hop(own, s1, s1_sem, kv, sibling).wait_send()
        hop(a1, s2, s2_sem, kv, sibling).wait_send()


def local(queries, cache_keys, cache_values, stretch_keys, stretch_values, verticals, slashes):
    smem = pl.BlockSpec(memory_space=pltpu.SMEM)
    hbm = pl.BlockSpec(memory_space=pl.ANY)
    dma = pltpu.SemaphoreType.DMA
    vmem = pltpu.VMEM
    return pl.pallas_call(
        kernel,
        out_shape=jax.ShapeDtypeStruct((GROUP, QROWS, HD), BF16),
        in_specs=[smem, smem] + [hbm] * 5,
        out_specs=hbm,
        scratch_shapes=[
            vmem((GROUP, QROWS, HD), BF16),
            vmem((2, CB, BLK, HD), BF16),
            vmem((2, (SPAN + 1) * QB, BLK, HD), BF16),
            vmem((2, BLK, HD), BF16),
            vmem((NY, QUARTER, HD), BF16),
            vmem((2, NY, QUARTER, HD), BF16),
            vmem((NY, QUARTER, HD), BF16),
            vmem((NY, QUARTER, HD), BF16),
            vmem((3, QUARTER, HD), BF16),
            vmem((3, QUARTER, HD), BF16),
            vmem((2, NY, QUARTER, HD), BF16),
            vmem((NY * QUARTER, 2 * HD), BF16),
            vmem((QB, (SPAN + 1) * BLK, HD), BF16),
            vmem((QB, (SPAN + 1) * BLK, 2 * HD), BF16),
            vmem((GROUP, QROWS, 2 * HD), F32),
            vmem((GROUP, QROWS, HD), F32),
            vmem((GROUP, QROWS, HD), BF16),
            dma((5,)),
            dma((GROUP,)),
            dma((2,)),
            dma((6,)),
            dma((4,)),
            dma((4,)),
            dma((6,)),
            dma((2 * NY,)),
            dma((4,)),
            dma((4,)),
            dma((4,)),
            dma((4,)),
        ],
        compiler_params=pltpu.CompilerParams(collective_id=0, has_side_effects=True, vmem_limit_bytes=60 * 2**20),
        cost_estimate=pl.CostEstimate(flops=3500000000, bytes_accessed=4000000, transcendentals=7000000),
        name="sparse_attention",
    )(
        verticals,
        slashes,
        queries,
        cache_keys.reshape(CB, BLK, HD),
        cache_values.reshape(CB, BLK, HD),
        stretch_keys.reshape(QB, BLK, HD),
        stretch_values.reshape(QB, BLK, HD),
    )


def solution(mesh):
    return jax.shard_map(
        local,
        mesh=mesh,
        in_specs=(
            P("head", "ctx", None),
            P("head", "ctx", None),
            P("head", "ctx", None),
            P("head", "ctx", None),
            P("head", "ctx", None),
            P("head", None),
            P("head", None),
        ),
        out_specs=P("head", "ctx", None),
        check_vma=False,
    )
```

```python
import math

import jax
import jax.numpy as jnp
from jax import lax
from jax.experimental import pallas as pl
from jax.experimental.pallas import tpu as pltpu
from jax.sharding import PartitionSpec as P

BLK = 128
HD = 128
NV = 8
SPAN = 4
GROUP = 4
NY, NZ = 4, 8
LAST = 2 * NY * NZ
QROWS = 1024
QB = QROWS // BLK
CROWS = 2048
CB = CROWS // BLK
LASTBLOCK = LAST * CB - 1
PART = BLK // NY
FREE = 5
FIXED = NV - FREE
FROWS = FREE * PART
SROWS = FIXED * PART
MESH = pl.DeviceIdType.MESH
COEF = math.log2(math.e) / math.sqrt(HD)
F32 = jnp.float32
BF16 = jnp.bfloat16


def tile(q, k, v, m, acc, keep=None):
    scores = lax.dot_general(q, k, (((1,), (1,)), ((), ())), preferred_element_type=F32)
    if keep is not None:
        scores = jnp.where(keep, scores, -jnp.inf)
    top = jnp.max(scores, axis=1, keepdims=True)
    new = top if m is None else jnp.maximum(m, top)
    p = jnp.exp2((scores - new) * COEF).astype(BF16)
    o = jnp.dot(p, v, preferred_element_type=F32)
    if m is not None:
        o = acc * jnp.exp2((m - new) * COEF) + o
    return new, o


def one_if(lo, hi, x):
    return jnp.minimum(jnp.maximum(x - (lo - 1), 0), 1) * jnp.minimum(jnp.maximum(hi + 1 - x, 0), 1)


def sort_listed(verts):
    listed = [verts[0, j] for j in range(NV)]
    free = [one_if(CB, LASTBLOCK - 1, v) for v in listed]
    at = [0] * FREE
    count = 0
    for v, is_free in zip(listed, free):
        for t in range(FREE):
            at[t] = at[t] + v * is_free * one_if(t, t, count)
        count = count + is_free
    low = 0
    for v in listed:
        low = low + v * one_if(1, CB - 1, v)
    return at, low


def kernel(
    verts, slashes, q_hbm, ck_hbm, cv_hbm, sk_hbm, sv_hbm, out_hbm,
    q_v, cache, near, older, gate, offer, pair, mixed, yb, zb1, zb2, far, fixed,
    far_k, far_v, fix_k, fix_v, near_k, near_v, old_k, old_v, acc_s, max_s, out_v,
    in_sem, out_sem, pair_sem, y_sem, z1_sem, z2_sem, ag_sem, fs_sem,
    fy_sem, fz0_sem, fz7_sem, fg_sem, ff_sem, a1_sem, a2_sem, s1_sem, s2_sem,
):
    me = lax.axis_index("ctx")
    c = lax.rem(me, 2)
    z = lax.rem(lax.div(me, 2), NZ)
    y = lax.div(me, 2 * NZ)

    def at(yy, zz, cc):
        return {"ctx": (yy * NZ + zz) * 2 + cc}

    sibling = at(y, z, 1 - c)
    y_peer = [at(lax.rem(y + k, NY), z, c) for k in range(1, NY)]
    z_peer = [at(y, lax.rem(z + k, NZ), c) for k in range(NZ)]
    ahead = {"ctx": lax.rem(me + 2, LAST)}
    behind = {"ctx": lax.rem(me - 2 + LAST, LAST)}
    a1, s1, own = (near.at[:, i * QB : (i + 1) * QB] for i in range(3))
    a2, s2 = (older.at[:, i * QB : (i + 1) * QB] for i in range(2))
    sends = me + 2 < LAST
    gets1 = me >= 2
    gets2 = me >= 4
    first_z = z == 0
    last_z = z == NZ - 1

    loads = [
        pltpu.make_async_copy(ck_hbm, cache.at[0], in_sem.at[0]),
        pltpu.make_async_copy(cv_hbm, cache.at[1], in_sem.at[1]),
        pltpu.make_async_copy(sk_hbm, own.at[0], in_sem.at[2]),
        pltpu.make_async_copy(sv_hbm, own.at[1], in_sem.at[3]),
        pltpu.make_async_copy(q_hbm, q_v, in_sem.at[4]),
    ]
    for load in loads:
        load.start()

    barrier = pltpu.get_barrier_semaphore()
    peers = [sibling] + y_peer + z_peer[1:] + [ahead, behind]
    for peer in peers:
        pl.semaphore_signal(barrier, inc=1, device_id=peer, device_id_type=MESH)

    free, low = sort_listed(verts)
    offered = [lax.rem(v, CB) for v in free] + [0, low, CB - 1]

    def part(j):
        return slice(j * PART, (j + 1) * PART)

    loads[0].wait()
    loads[1].wait()
    for j, block in enumerate(offered):
        pair[pl.ds(c, 1), :, part(j), :] = cache[pl.ds(c, 1), pl.ds(block, 1)].reshape(1, NY, PART, HD)
        offer[:, part(j), :] = cache[pl.ds(1 - c, 1), pl.ds(block, 1)].reshape(NY, PART, HD)
    pl.semaphore_wait(barrier, len(peers))

    def remote(src, dst, send_sem, recv_sem, to):
        return pltpu.make_async_remote_copy(
            src_ref=src, dst_ref=dst, send_sem=send_sem, recv_sem=recv_sem, device_id=to, device_id_type=MESH
        )

    pair_out = remote(offer, pair.at[c], pair_sem.at[0], pair_sem.at[1], sibling)
    pair_out.start()
    loads[2].wait()
    loads[3].wait()

    def hop(src, dst, sem, kv, to):
        return remote(src.at[kv], dst.at[kv], sem.at[kv], sem.at[2 + kv], to)

    @pl.when(sends)
    def _():
        for kv in (0, 1):
            hop(own, a1, a1_sem, kv, ahead).start()

    @pl.when(jnp.logical_not(gets1))
    def _():
        near[:, :QB] = jnp.zeros((2, QB, BLK, HD), BF16)

    @pl.when(jnp.logical_not(gets2))
    def _():
        older[:, :QB] = jnp.zeros((2, QB, BLK, HD), BF16)

    gate[0] = jnp.zeros((BLK, HD), BF16)
    gate[1] = jnp.ones((BLK, HD), BF16)
    far_v[:, HD:] = jnp.ones((NY * FROWS, HD), BF16)
    fix_v[:, HD:] = jnp.ones((NY * SROWS, HD), BF16)

    owner = [lax.div(v, CB) for v in free]
    owner_y = [lax.div(d, 2 * NZ) for d in owner]
    owner_z = [lax.rem(lax.div(d, 2), NZ) for d in owner]
    owner_c = [lax.rem(d, 2) for d in owner]

    remote(offer, pair.at[1 - c], pair_sem.at[0], pair_sem.at[1], sibling).wait_recv()
    for j in range(FREE):
        mixed[:, part(j), :] = pair[pl.ds(owner_c[j], 1), :, part(j), :][0]
    y_out = []
    for k in range(1, NY):
        to = lax.rem(y + k, NY)
        y_out.append(
            remote(mixed.at[to, :FROWS], yb.at[y], y_sem.at[k - 1], y_sem.at[2 + k], y_peer[k - 1])
        )
        y_out[-1].start()
    yb[pl.ds(y, 1)] = mixed[pl.ds(y, 1), :FROWS, :]
    mixed[:, FROWS : FROWS + 2 * PART, :] = pair[0, :, FROWS : FROWS + 2 * PART, :]
    mixed[:, FROWS + 2 * PART :, :] = pair[1, :, FROWS + 2 * PART :, :]

    @pl.when(c == 0)
    def _():
        for kv in (0, 1):
            hop(own, s1, s1_sem, kv, sibling).start()

    halves = (
        (jnp.logical_and(first_z, y == 0), first_z, 0, 2 * PART, fz0_sem),
        (jnp.logical_and(last_z, y == NY - 1), last_z, 2 * PART, SROWS, fz7_sem),
    )

    def fixed_y(k, lo, hi):
        to = lax.rem(y + k, NY)
        return remote(
            mixed.at[to, FROWS + lo : FROWS + hi], fixed.at[c, to, lo:hi], fy_sem.at[k - 1], fy_sem.at[3], y_peer[k - 1]
        )

    def fixed_z(k, lo, hi, sem):
        return remote(fixed.at[c, y, lo:hi], fixed.at[c, y, lo:hi], sem.at[k], sem.at[0], z_peer[k])

    for root, line, lo, hi, sem in halves:

        @pl.when(root)
        def _():
            for k in range(1, NY):
                fixed_y(k, lo, hi).start()
            fixed[pl.ds(c, 1), pl.ds(y, 1), lo:hi, :] = mixed[pl.ds(y, 1), FROWS + lo : FROWS + hi, :][None]

    for k in range(1, NY):
        frm = lax.rem(y + NY - k, NY)
        remote(mixed.at[frm, :FROWS], yb.at[frm], y_sem.at[k - 1], y_sem.at[2 + k], y_peer[k - 1]).wait_recv()
    for j in range(FREE):
        zb1[1, part(j), :] = yb[pl.ds(owner_y[j], 1), part(j), :][0]
    z1_out = [
        remote(zb1.at[1], zb1.at[0], z1_sem.at[0], z1_sem.at[2], z_peer[1]),
        remote(zb1.at[1], zb1.at[2], z1_sem.at[1], z1_sem.at[3], z_peer[NZ - 1]),
    ]
    for copy in z1_out:
        copy.start()

    for root, line, lo, hi, sem in halves:

        @pl.when(jnp.logical_and(line, jnp.logical_not(root)))
        def _():
            fixed_y(1, lo, hi).wait_recv()

        @pl.when(line)
        def _():
            for k in range(1, NZ):
                fixed_z(k, lo, hi, sem).start()

    for copy in z1_out:
        copy.wait_recv()
    off = [lax.rem(o - z + NZ, NZ) for o in owner_z]
    for j in range(FREE):
        slot = 1 + one_if(1, 1, off[j]) - one_if(NZ - 1, NZ - 1, off[j])
        zb2[1, part(j), :] = zb1[pl.ds(slot, 1), part(j), :][0]
    z2_out = [
        remote(zb2.at[1], zb2.at[0], z2_sem.at[0], z2_sem.at[2], z_peer[3]),
        remote(zb2.at[1], zb2.at[2], z2_sem.at[1], z2_sem.at[3], z_peer[NZ - 3]),
    ]
    for copy in z2_out:
        copy.start()

    for root, line, lo, hi, sem in halves:

        @pl.when(jnp.logical_not(line))
        def _():
            fixed_z(1, lo, hi, sem).wait_recv()

    def gather(buf, sem, k):
        return remote(buf.at[c, y], buf.at[c, y], sem.at[k - 1], sem.at[2 + k], y_peer[k - 1])

    def gathered(buf, sem, k):
        frm = lax.rem(y + NY - k, NY)
        return remote(buf.at[c, frm], buf.at[c, frm], sem.at[k - 1], sem.at[2 + k], y_peer[k - 1])

    def share(buf, sem, k):
        frm = lax.rem(y + NY - k, NY)
        return remote(buf.at[c, frm], buf.at[c, frm], sem.at[k], sem.at[NY + k], sibling)

    def shared(buf, sem, k):
        frm = lax.rem(y + NY - k, NY)
        return remote(buf.at[1 - c, frm], buf.at[1 - c, frm], sem.at[k], sem.at[NY + k], sibling)

    for k in range(1, NY):
        gather(fixed, fg_sem, k).start()
    share(fixed, ff_sem, 0).start()

    for kv in (0, 1):

        @pl.when(gets1)
        def _():
            hop(own, a1, a1_sem, kv, behind).wait_recv()

        @pl.when(c == 0)
        def _():
            hop(a1, s2, s2_sem, kv, sibling).start()

        @pl.when(c == 1)
        def _():
            hop(a1, s1, s1_sem, kv, sibling).start()

    for k in range(1, NY):
        gathered(fixed, fg_sem, k).wait_recv()
        share(fixed, ff_sem, k).start()

    for copy in z2_out:
        copy.wait_recv()
    for j in range(FREE):
        slot = 1 + one_if(2, 4, off[j]) - one_if(5, 6, off[j])
        far[pl.ds(c, 1), pl.ds(y, 1), part(j), :] = zb2[pl.ds(slot, 1), part(j), :][None]
    for k in range(1, NY):
        gather(far, ag_sem, k).start()
    share(far, fs_sem, 0).start()

    @pl.when(jnp.logical_and(gets1, sends))
    def _():
        for kv in (0, 1):
            hop(a1, a2, a2_sem, kv, ahead).start()

    loads[4].wait()
    for kv in (0, 1):
        hop(own, s1, s1_sem, kv, sibling).wait_recv()
    for k in range(NY):
        shared(fixed, ff_sem, k).wait_recv()
    fix_k[...] = fixed[0].reshape(NY * SROWS, HD)
    fix_v[:, :HD] = fixed[1].reshape(NY * SROWS, HD)
    older[:, 2 * QB :] = near[:, :QB]

    def diagonal(b, i, ring, offset, k_ref, v_ref, rows):
        s = slashes[0, i]
        counts = jnp.minimum(jnp.maximum(me * QB + b - s + 1, 0), 1)
        yes = gate[pl.ds(counts, 1)][0]
        no = gate[pl.ds(1 - counts, 1)][0]
        head_row = jnp.broadcast_to(near[0, 2 * QB + b, 0:16, :][0:1], (BLK, HD))
        block = pl.ds(jnp.minimum(jnp.maximum(offset + b - s, 0), 3 * QB - 1), 1)
        k_ref[b, rows, :] = ring[0, block][0] * yes + head_row * no
        v_ref[b, rows, :HD] = ring[1, block][0] * yes
        v_ref[b, rows, HD:] = yes

    def block_rows(b):
        return pl.ds(pl.multiple_of(b * BLK, BLK), BLK)

    def near_block(b, _):
        diagonal(b, 0, near, 2 * QB, near_k, near_v, slice(0, BLK))
        diagonal(b, 1, near, 2 * QB, near_k, near_v, slice(BLK, 2 * BLK))
        near_k[b, 2 * BLK : 3 * BLK, :] = near[0, 2 * QB + b]
        near_v[b, 2 * BLK : 3 * BLK, :HD] = near[1, 2 * QB + b]
        near_v[b, 2 * BLK : 3 * BLK, HD:] = jnp.ones((BLK, HD), BF16)
        near_k[b, 3 * BLK :, :] = fix_k[:BLK, :]
        near_v[b, 3 * BLK :, :] = fix_v[:BLK, :]
        q = q_v[:, block_rows(b), :].reshape(GROUP * BLK, HD)
        t = lax.rem(lax.broadcasted_iota(jnp.int32, (GROUP * BLK, 2 * BLK), 0), BLK)
        u = lax.broadcasted_iota(jnp.int32, (GROUP * BLK, 2 * BLK), 1)
        keep = jnp.logical_or(u <= t, u >= BLK)
        m, acc = tile(q, near_k[b, 2 * BLK :, :], near_v[b, 2 * BLK :, :], None, None, keep)
        m, acc = tile(q, near_k[b, : 2 * BLK, :], near_v[b, : 2 * BLK, :], m, acc)
        m, acc = tile(q, fix_k[BLK:, :], fix_v[BLK:, :], m, acc)
        acc_s[:, block_rows(b), :] = acc.reshape(GROUP, BLK, 2 * HD)
        max_s[:, block_rows(b), :] = jnp.broadcast_to(m, (GROUP * BLK, HD)).reshape(GROUP, BLK, HD)
        return 0

    lax.fori_loop(0, QB, near_block, 0, unroll=True)

    for k in range(1, NY):
        gathered(far, ag_sem, k).wait_recv()
        share(far, fs_sem, k).start()
    for k in range(NY):
        shared(far, fs_sem, k).wait_recv()
    far_k[...] = far[0].reshape(NY * FROWS, HD)
    far_v[:, :HD] = far[1].reshape(NY * FROWS, HD)

    def far_head(h, _):
        q = q_v[h]
        m, acc = jnp.max(max_s[h], axis=1, keepdims=True), acc_s[h]
        for lo in range(0, NY * FROWS, 2 * BLK):
            hi = min(lo + 2 * BLK, NY * FROWS)
            m, acc = tile(q, far_k[lo:hi, :], far_v[lo:hi, :], m, acc)
        acc_s[h] = acc
        max_s[h] = jnp.broadcast_to(m, (QROWS, HD))
        return 0

    lax.fori_loop(0, GROUP, far_head, 0, unroll=True)

    for kv in (0, 1):

        @pl.when(gets2)
        def _():
            hop(a1, a2, a2_sem, kv, behind).wait_recv()

        @pl.when(c == 1)
        def _():
            hop(a2, s2, s2_sem, kv, sibling).start()

    for kv in (0, 1):
        hop(a1, s2, s2_sem, kv, sibling).wait_recv()

    def old_block(b, _):
        diagonal(b, 2, older, SPAN * QB, old_k, old_v, slice(0, BLK))
        diagonal(b, 3, older, SPAN * QB, old_k, old_v, slice(BLK, 2 * BLK))
        rows = block_rows(b)
        q = q_v[:, rows, :].reshape(GROUP * BLK, HD)
        m = jnp.max(max_s[:, rows, :].reshape(GROUP * BLK, HD), axis=1, keepdims=True)
        m, acc = tile(q, old_k[b], old_v[b], m, acc_s[:, rows, :].reshape(GROUP * BLK, 2 * HD))
        out_v[:, rows, :] = (acc[:, :HD] / acc[:, HD:]).astype(BF16).reshape(GROUP, BLK, HD)
        pltpu.make_async_copy(out_v.at[:, rows], out_hbm.at[:, rows], out_sem.at[b]).start()
        return 0

    lax.fori_loop(0, QB, old_block, 0, unroll=True)

    for b in range(QB):
        rows = pl.ds(b * BLK, BLK)
        pltpu.make_async_copy(out_v.at[:, rows], out_hbm.at[:, rows], out_sem.at[b]).wait()
    for copy in [pair_out] + y_out + z1_out + z2_out:
        copy.wait_send()
    for k in range(1, NY):
        gather(fixed, fg_sem, k).wait_send()
        gather(far, ag_sem, k).wait_send()
    for k in range(NY):
        share(fixed, ff_sem, k).wait_send()
        share(far, fs_sem, k).wait_send()
    for root, line, lo, hi, sem in halves:

        @pl.when(root)
        def _():
            for k in range(1, NY):
                fixed_y(k, lo, hi).wait_send()

        @pl.when(line)
        def _():
            for k in range(1, NZ):
                fixed_z(k, lo, hi, sem).wait_send()

    for kv in (0, 1):

        @pl.when(sends)
        def _():
            hop(own, a1, a1_sem, kv, ahead).wait_send()

        @pl.when(jnp.logical_and(gets1, sends))
        def _():
            hop(a1, a2, a2_sem, kv, ahead).wait_send()

        hop(own, s1, s1_sem, kv, sibling).wait_send()
        hop(a1, s2, s2_sem, kv, sibling).wait_send()


def local(queries, cache_keys, cache_values, stretch_keys, stretch_values, verticals, slashes):
    smem = pl.BlockSpec(memory_space=pltpu.SMEM)
    hbm = pl.BlockSpec(memory_space=pl.ANY)
    dma = pltpu.SemaphoreType.DMA
    vmem = pltpu.VMEM
    return pl.pallas_call(
        kernel,
        out_shape=jax.ShapeDtypeStruct((GROUP, QROWS, HD), BF16),
        in_specs=[smem, smem] + [hbm] * 5,
        out_specs=hbm,
        scratch_shapes=[
            vmem((GROUP, QROWS, HD), BF16),
            vmem((2, CB, BLK, HD), BF16),
            vmem((2, 3 * QB, BLK, HD), BF16),
            vmem((2, 3 * QB, BLK, HD), BF16),
            vmem((2, BLK, HD), BF16),
            vmem((NY, NV * PART, HD), BF16),
            vmem((2, NY, NV * PART, HD), BF16),
            vmem((NY, NV * PART, HD), BF16),
            vmem((NY, FROWS, HD), BF16),
            vmem((3, FROWS, HD), BF16),
            vmem((3, FROWS, HD), BF16),
            vmem((2, NY, FROWS, HD), BF16),
            vmem((2, NY, SROWS, HD), BF16),
            vmem((NY * FROWS, HD), BF16),
            vmem((NY * FROWS, 2 * HD), BF16),
            vmem((NY * SROWS, HD), BF16),
            vmem((NY * SROWS, 2 * HD), BF16),
            vmem((QB, 4 * BLK, HD), BF16),
            vmem((QB, 4 * BLK, 2 * HD), BF16),
            vmem((QB, 2 * BLK, HD), BF16),
            vmem((QB, 2 * BLK, 2 * HD), BF16),
            vmem((GROUP, QROWS, 2 * HD), F32),
            vmem((GROUP, QROWS, HD), F32),
            vmem((GROUP, QROWS, HD), BF16),
            dma((5,)),
            dma((QB,)),
            dma((2,)),
            dma((6,)),
            dma((4,)),
            dma((4,)),
            dma((6,)),
            dma((2 * NY,)),
            dma((4,)),
            dma((NZ,)),
            dma((NZ,)),
            dma((6,)),
            dma((2 * NY,)),
            dma((4,)),
            dma((4,)),
            dma((4,)),
            dma((4,)),
        ],
        compiler_params=pltpu.CompilerParams(collective_id=0, has_side_effects=True, vmem_limit_bytes=60 * 2**20),
        cost_estimate=pl.CostEstimate(flops=3500000000, bytes_accessed=4000000, transcendentals=7000000),
        name="sparse_attention",
    )(
        verticals,
        slashes,
        queries,
        cache_keys.reshape(CB, BLK, HD),
        cache_values.reshape(CB, BLK, HD),
        stretch_keys.reshape(QB, BLK, HD),
        stretch_values.reshape(QB, BLK, HD),
    )


def solution(mesh):
    return jax.shard_map(
        local,
        mesh=mesh,
        in_specs=(
            P("head", "ctx", None),
            P("head", "ctx", None),
            P("head", "ctx", None),
            P("head", "ctx", None),
            P("head", "ctx", None),
            P("head", None),
            P("head", None),
        ),
        out_specs=P("head", "ctx", None),
        check_vma=False,
    )
```

```python
import math

import jax
import jax.numpy as jnp
from jax import lax
from jax.experimental import pallas as pl
from jax.experimental.pallas import tpu as pltpu
from jax.sharding import PartitionSpec as P

BLK = 128
HD = 128
NV = 8
SPAN = 4
GROUP = 4
NY, NZ = 4, 8
LAST = 2 * NY * NZ
QROWS = 1024
QB = QROWS // BLK
CROWS = 2048
CB = CROWS // BLK
LASTBLOCK = LAST * CB - 1
PART = BLK // NY
FREE = 5
FIXED = NV - FREE
FROWS = FREE * PART
SROWS = FIXED * PART
MESH = pl.DeviceIdType.MESH
COEF = math.log2(math.e) / math.sqrt(HD)
F32 = jnp.float32
BF16 = jnp.bfloat16


def tile(q, k, v, m, acc, keep=None):
    scores = lax.dot_general(q, k, (((1,), (1,)), ((), ())), preferred_element_type=F32)
    if keep is not None:
        scores = jnp.where(keep, scores, -jnp.inf)
    top = jnp.max(scores, axis=1, keepdims=True)
    new = top if m is None else jnp.maximum(m, top)
    p = jnp.exp2((scores - new) * COEF).astype(BF16)
    o = jnp.dot(p, v, preferred_element_type=F32)
    if m is not None:
        o = acc * jnp.exp2((m - new) * COEF) + o
    return new, o


def one_if(lo, hi, x):
    return jnp.minimum(jnp.maximum(x - (lo - 1), 0), 1) * jnp.minimum(jnp.maximum(hi + 1 - x, 0), 1)


def sort_listed(verts):
    listed = [verts[0, j] for j in range(NV)]
    free = [one_if(CB, LASTBLOCK - 1, v) for v in listed]
    at = [0] * FREE
    count = 0
    for v, is_free in zip(listed, free):
        for t in range(FREE):
            at[t] = at[t] + v * is_free * one_if(t, t, count)
        count = count + is_free
    low = 0
    for v in listed:
        low = low + v * one_if(1, CB - 1, v)
    return at, low


def kernel(
    verts, slashes, q_hbm, ck_hbm, cv_hbm, sk_hbm, sv_hbm, out_hbm,
    q_v, cache, near, older, stop, gate, offer, pair, mixed, yb, zb1, zb2, far, fixed,
    far_k, far_v, fix_k, fix_v, near_k, near_v, old_k, old_v, acc_s, max_s, out_v,
    in_sem, out_sem, pair_sem, y_sem, z1_sem, z2_sem, ag_sem, fs_sem,
    fy_sem, fz0_sem, fz7_sem, fg_sem, ff_sem, a1_sem, a2_sem, s1_sem, s2_sem, stop_sem,
):
    me = lax.axis_index("ctx")
    c = lax.rem(me, 2)
    z = lax.rem(lax.div(me, 2), NZ)
    y = lax.div(me, 2 * NZ)

    def at(yy, zz, cc):
        return {"ctx": (yy * NZ + zz) * 2 + cc}

    sibling = at(y, z, 1 - c)
    y_peer = [at(lax.rem(y + k, NY), z, c) for k in range(1, NY)]
    z_peer = [at(y, lax.rem(z + k, NZ), c) for k in range(NZ)]
    ahead = {"ctx": lax.rem(me + 2, LAST)}
    behind = {"ctx": lax.rem(me - 2 + LAST, LAST)}
    a1, s1, own = (near.at[:, i * QB : (i + 1) * QB] for i in range(3))
    a2, s2 = (older.at[:, i * QB : (i + 1) * QB] for i in range(2))
    sends = me + 2 < LAST
    gets1 = me >= 2
    gets2 = me >= 4
    first_z = z == 0
    last_z = z == NZ - 1

    loads = [
        pltpu.make_async_copy(ck_hbm, cache.at[0], in_sem.at[0]),
        pltpu.make_async_copy(cv_hbm, cache.at[1], in_sem.at[1]),
        pltpu.make_async_copy(sk_hbm, own.at[0], in_sem.at[2]),
        pltpu.make_async_copy(sv_hbm, own.at[1], in_sem.at[3]),
        pltpu.make_async_copy(q_hbm, q_v, in_sem.at[4]),
    ]
    for load in loads:
        load.start()

    barrier = pltpu.get_barrier_semaphore()
    peers = [sibling] + y_peer + z_peer[1:] + [ahead, behind]
    for peer in peers:
        pl.semaphore_signal(barrier, inc=1, device_id=peer, device_id_type=MESH)

    free, low = sort_listed(verts)
    offered = [lax.rem(v, CB) for v in free] + [0, low, CB - 1]

    def part(j):
        return slice(j * PART, (j + 1) * PART)

    loads[0].wait()
    loads[1].wait()
    for j, block in enumerate(offered):
        pair[pl.ds(c, 1), :, part(j), :] = cache[pl.ds(c, 1), pl.ds(block, 1)].reshape(1, NY, PART, HD)
        offer[:, part(j), :] = cache[pl.ds(1 - c, 1), pl.ds(block, 1)].reshape(NY, PART, HD)
    pl.semaphore_wait(barrier, len(peers))

    def remote(src, dst, send_sem, recv_sem, to):
        return pltpu.make_async_remote_copy(
            src_ref=src, dst_ref=dst, send_sem=send_sem, recv_sem=recv_sem, device_id=to, device_id_type=MESH
        )

    pair_out = remote(offer, pair.at[c], pair_sem.at[0], pair_sem.at[1], sibling)
    pair_out.start()
    loads[2].wait()
    loads[3].wait()

    def hop(src, dst, sem, kv, to):
        return remote(src.at[kv], dst.at[kv], sem.at[kv], sem.at[2 + kv], to)

    in_row = z < NZ - 1
    leaves_row = jnp.logical_and(last_z, sends)
    passes_keys = jnp.logical_and(first_z, y < NY - 1)
    passes_values = jnp.logical_and(last_z, y > 0)
    corner = (z_peer[1], y_peer[0])

    def leg1(i, kv):
        return remote((own, a1)[i].at[kv], stop.at[i], (a1_sem, a2_sem)[i].at[kv], stop_sem.at[i], corner[kv])

    def leg2(i, kv):
        sem = (a1_sem, a2_sem)[i].at[2 + kv]
        return remote(stop.at[i], (a1, a2)[i].at[kv], stop_sem.at[2 + i], sem, corner[1 - kv])

    def stretch_step(step):
        for kv in (0, 1):
            if step == 0:

                @pl.when(jnp.logical_and(sends, in_row))
                def _():
                    hop(own, a1, a1_sem, kv, ahead).start()

            if step == 0:

                @pl.when(leaves_row)
                def _():
                    leg1(0, kv).start()

            if step == (1, 2)[kv]:

                @pl.when((passes_keys, passes_values)[kv])
                def _():
                    leg1(0, kv).wait_recv()
                    leg2(0, kv).start()

            if step == 4:

                @pl.when(gets1)
                def _():
                    hop(own, a1, a1_sem, kv, behind).wait_recv()

                @pl.when(c == 0)
                def _():
                    hop(a1, s2, s2_sem, kv, sibling).start()

                @pl.when(c == 1)
                def _():
                    hop(a1, s1, s1_sem, kv, sibling).start()

                @pl.when(jnp.logical_and(gets1, in_row))
                def _():
                    hop(a1, a2, a2_sem, kv, ahead).start()

                @pl.when(leaves_row)
                def _():
                    leg1(1, kv).start()

            if step == 5:

                @pl.when((passes_keys, passes_values)[kv])
                def _():
                    leg1(1, kv).wait_recv()
                    leg2(1, kv).start()

    stretch_step(0)

    @pl.when(jnp.logical_not(gets1))
    def _():
        near[:, :QB] = jnp.zeros((2, QB, BLK, HD), BF16)

    @pl.when(jnp.logical_not(gets2))
    def _():
        older[:, :QB] = jnp.zeros((2, QB, BLK, HD), BF16)

    gate[0] = jnp.zeros((BLK, HD), BF16)
    gate[1] = jnp.ones((BLK, HD), BF16)
    far_v[:, HD:] = jnp.ones((NY * FROWS, HD), BF16)
    fix_v[:, HD:] = jnp.ones((NY * SROWS, HD), BF16)

    owner = [lax.div(v, CB) for v in free]
    owner_y = [lax.div(d, 2 * NZ) for d in owner]
    owner_z = [lax.rem(lax.div(d, 2), NZ) for d in owner]
    owner_c = [lax.rem(d, 2) for d in owner]

    remote(offer, pair.at[1 - c], pair_sem.at[0], pair_sem.at[1], sibling).wait_recv()
    for j in range(FREE):
        mixed[:, part(j), :] = pair[pl.ds(owner_c[j], 1), :, part(j), :][0]
    y_out = []
    for k in range(1, NY):
        to = lax.rem(y + k, NY)
        y_out.append(
            remote(mixed.at[to, :FROWS], yb.at[y], y_sem.at[k - 1], y_sem.at[2 + k], y_peer[k - 1])
        )
        y_out[-1].start()
    yb[pl.ds(y, 1)] = mixed[pl.ds(y, 1), :FROWS, :]
    mixed[:, FROWS : FROWS + 2 * PART, :] = pair[0, :, FROWS : FROWS + 2 * PART, :]
    mixed[:, FROWS + 2 * PART :, :] = pair[1, :, FROWS + 2 * PART :, :]

    @pl.when(c == 0)
    def _():
        for kv in (0, 1):
            hop(own, s1, s1_sem, kv, sibling).start()

    halves = (
        (jnp.logical_and(first_z, y == 0), first_z, 0, 2 * PART, fz0_sem),
        (jnp.logical_and(last_z, y == NY - 1), last_z, 2 * PART, SROWS, fz7_sem),
    )

    def fixed_y(k, lo, hi):
        to = lax.rem(y + k, NY)
        return remote(
            mixed.at[to, FROWS + lo : FROWS + hi], fixed.at[c, to, lo:hi], fy_sem.at[k - 1], fy_sem.at[3], y_peer[k - 1]
        )

    def fixed_z(k, lo, hi, sem):
        return remote(fixed.at[c, y, lo:hi], fixed.at[c, y, lo:hi], sem.at[k], sem.at[0], z_peer[k])

    for root, line, lo, hi, sem in halves:

        @pl.when(root)
        def _():
            for k in range(1, NY):
                fixed_y(k, lo, hi).start()
            fixed[pl.ds(c, 1), pl.ds(y, 1), lo:hi, :] = mixed[pl.ds(y, 1), FROWS + lo : FROWS + hi, :][None]

    for k in range(1, NY):
        frm = lax.rem(y + NY - k, NY)
        remote(mixed.at[frm, :FROWS], yb.at[frm], y_sem.at[k - 1], y_sem.at[2 + k], y_peer[k - 1]).wait_recv()
    stretch_step(1)
    for j in range(FREE):
        zb1[1, part(j), :] = yb[pl.ds(owner_y[j], 1), part(j), :][0]
    z1_out = [
        remote(zb1.at[1], zb1.at[0], z1_sem.at[0], z1_sem.at[2], z_peer[1]),
        remote(zb1.at[1], zb1.at[2], z1_sem.at[1], z1_sem.at[3], z_peer[NZ - 1]),
    ]
    for copy in z1_out:
        copy.start()

    for root, line, lo, hi, sem in halves:

        @pl.when(jnp.logical_and(line, jnp.logical_not(root)))
        def _():
            fixed_y(1, lo, hi).wait_recv()

        @pl.when(line)
        def _():
            for k in range(1, NZ):
                fixed_z(k, lo, hi, sem).start()

    for copy in z1_out:
        copy.wait_recv()
    stretch_step(2)
    off = [lax.rem(o - z + NZ, NZ) for o in owner_z]
    for j in range(FREE):
        slot = 1 + one_if(1, 1, off[j]) - one_if(NZ - 1, NZ - 1, off[j])
        zb2[1, part(j), :] = zb1[pl.ds(slot, 1), part(j), :][0]
    z2_out = [
        remote(zb2.at[1], zb2.at[0], z2_sem.at[0], z2_sem.at[2], z_peer[3]),
        remote(zb2.at[1], zb2.at[2], z2_sem.at[1], z2_sem.at[3], z_peer[NZ - 3]),
    ]
    for copy in z2_out:
        copy.start()

    for root, line, lo, hi, sem in halves:

        @pl.when(jnp.logical_not(line))
        def _():
            fixed_z(1, lo, hi, sem).wait_recv()

    def gather(buf, sem, k):
        return remote(buf.at[c, y], buf.at[c, y], sem.at[k - 1], sem.at[2 + k], y_peer[k - 1])

    def gathered(buf, sem, k):
        frm = lax.rem(y + NY - k, NY)
        return remote(buf.at[c, frm], buf.at[c, frm], sem.at[k - 1], sem.at[2 + k], y_peer[k - 1])

    def share(buf, sem, k):
        frm = lax.rem(y + NY - k, NY)
        return remote(buf.at[c, frm], buf.at[c, frm], sem.at[k], sem.at[NY + k], sibling)

    def shared(buf, sem, k):
        frm = lax.rem(y + NY - k, NY)
        return remote(buf.at[1 - c, frm], buf.at[1 - c, frm], sem.at[k], sem.at[NY + k], sibling)

    for k in range(1, NY):
        gather(fixed, fg_sem, k).start()
    share(fixed, ff_sem, 0).start()

    for k in range(1, NY):
        gathered(fixed, fg_sem, k).wait_recv()
        share(fixed, ff_sem, k).start()

    for copy in z2_out:
        copy.wait_recv()
    for j in range(FREE):
        slot = 1 + one_if(2, 4, off[j]) - one_if(5, 6, off[j])
        far[pl.ds(c, 1), pl.ds(y, 1), part(j), :] = zb2[pl.ds(slot, 1), part(j), :][None]
    for k in range(1, NY):
        gather(far, ag_sem, k).start()
    share(far, fs_sem, 0).start()

    stretch_step(4)

    loads[4].wait()
    for kv in (0, 1):
        hop(own, s1, s1_sem, kv, sibling).wait_recv()
    for k in range(NY):
        shared(fixed, ff_sem, k).wait_recv()
    fix_k[...] = fixed[0].reshape(NY * SROWS, HD)
    fix_v[:, :HD] = fixed[1].reshape(NY * SROWS, HD)
    older[:, 2 * QB :] = near[:, :QB]

    def diagonal(b, i, ring, offset, k_ref, v_ref, rows):
        s = slashes[0, i]
        counts = jnp.minimum(jnp.maximum(me * QB + b - s + 1, 0), 1)
        yes = gate[pl.ds(counts, 1)][0]
        no = gate[pl.ds(1 - counts, 1)][0]
        head_row = jnp.broadcast_to(near[0, 2 * QB + b, 0:16, :][0:1], (BLK, HD))
        block = pl.ds(jnp.minimum(jnp.maximum(offset + b - s, 0), 3 * QB - 1), 1)
        k_ref[b, rows, :] = ring[0, block][0] * yes + head_row * no
        v_ref[b, rows, :HD] = ring[1, block][0] * yes
        v_ref[b, rows, HD:] = yes

    def block_rows(b):
        return pl.ds(pl.multiple_of(b * BLK, BLK), BLK)

    def near_block(b, _):
        diagonal(b, 0, near, 2 * QB, near_k, near_v, slice(0, BLK))
        diagonal(b, 1, near, 2 * QB, near_k, near_v, slice(BLK, 2 * BLK))
        near_k[b, 2 * BLK : 3 * BLK, :] = near[0, 2 * QB + b]
        near_v[b, 2 * BLK : 3 * BLK, :HD] = near[1, 2 * QB + b]
        near_v[b, 2 * BLK : 3 * BLK, HD:] = jnp.ones((BLK, HD), BF16)
        near_k[b, 3 * BLK :, :] = fix_k[:BLK, :]
        near_v[b, 3 * BLK :, :] = fix_v[:BLK, :]
        q = q_v[:, block_rows(b), :].reshape(GROUP * BLK, HD)
        t = lax.rem(lax.broadcasted_iota(jnp.int32, (GROUP * BLK, 2 * BLK), 0), BLK)
        u = lax.broadcasted_iota(jnp.int32, (GROUP * BLK, 2 * BLK), 1)
        keep = jnp.logical_or(u <= t, u >= BLK)
        m, acc = tile(q, near_k[b, 2 * BLK :, :], near_v[b, 2 * BLK :, :], None, None, keep)
        m, acc = tile(q, near_k[b, : 2 * BLK, :], near_v[b, : 2 * BLK, :], m, acc)
        m, acc = tile(q, fix_k[BLK:, :], fix_v[BLK:, :], m, acc)
        acc_s[:, block_rows(b), :] = acc.reshape(GROUP, BLK, 2 * HD)
        max_s[:, block_rows(b), :] = jnp.broadcast_to(m, (GROUP * BLK, HD)).reshape(GROUP, BLK, HD)
        return 0

    lax.fori_loop(0, QB, near_block, 0, unroll=True)

    for k in range(1, NY):
        gathered(far, ag_sem, k).wait_recv()
        share(far, fs_sem, k).start()
    stretch_step(5)
    for k in range(NY):
        shared(far, fs_sem, k).wait_recv()
    far_k[...] = far[0].reshape(NY * FROWS, HD)
    far_v[:, :HD] = far[1].reshape(NY * FROWS, HD)

    def far_head(h, _):
        q = q_v[h]
        m, acc = jnp.max(max_s[h], axis=1, keepdims=True), acc_s[h]
        for lo in range(0, NY * FROWS, 2 * BLK):
            hi = min(lo + 2 * BLK, NY * FROWS)
            m, acc = tile(q, far_k[lo:hi, :], far_v[lo:hi, :], m, acc)
        acc_s[h] = acc
        max_s[h] = jnp.broadcast_to(m, (QROWS, HD))
        return 0

    lax.fori_loop(0, GROUP, far_head, 0, unroll=True)

    for kv in (0, 1):

        @pl.when(gets2)
        def _():
            hop(a1, a2, a2_sem, kv, behind).wait_recv()

        @pl.when(c == 1)
        def _():
            hop(a2, s2, s2_sem, kv, sibling).start()

    for kv in (0, 1):
        hop(a1, s2, s2_sem, kv, sibling).wait_recv()

    def old_block(b, _):
        diagonal(b, 2, older, SPAN * QB, old_k, old_v, slice(0, BLK))
        diagonal(b, 3, older, SPAN * QB, old_k, old_v, slice(BLK, 2 * BLK))
        rows = block_rows(b)
        q = q_v[:, rows, :].reshape(GROUP * BLK, HD)
        m = jnp.max(max_s[:, rows, :].reshape(GROUP * BLK, HD), axis=1, keepdims=True)
        m, acc = tile(q, old_k[b], old_v[b], m, acc_s[:, rows, :].reshape(GROUP * BLK, 2 * HD))
        out_v[:, rows, :] = (acc[:, :HD] / acc[:, HD:]).astype(BF16).reshape(GROUP, BLK, HD)
        pltpu.make_async_copy(out_v.at[:, rows], out_hbm.at[:, rows], out_sem.at[b]).start()
        return 0

    lax.fori_loop(0, QB, old_block, 0, unroll=True)

    for b in range(QB):
        rows = pl.ds(b * BLK, BLK)
        pltpu.make_async_copy(out_v.at[:, rows], out_hbm.at[:, rows], out_sem.at[b]).wait()
    for copy in [pair_out] + y_out + z1_out + z2_out:
        copy.wait_send()
    for k in range(1, NY):
        gather(fixed, fg_sem, k).wait_send()
        gather(far, ag_sem, k).wait_send()
    for k in range(NY):
        share(fixed, ff_sem, k).wait_send()
        share(far, fs_sem, k).wait_send()
    for root, line, lo, hi, sem in halves:

        @pl.when(root)
        def _():
            for k in range(1, NY):
                fixed_y(k, lo, hi).wait_send()

        @pl.when(line)
        def _():
            for k in range(1, NZ):
                fixed_z(k, lo, hi, sem).wait_send()

    for kv in (0, 1):

        @pl.when(sends)
        def _():
            hop(own, a1, a1_sem, kv, ahead).wait_send()

        @pl.when(jnp.logical_and(gets1, sends))
        def _():
            hop(a1, a2, a2_sem, kv, ahead).wait_send()

        @pl.when((passes_keys, passes_values)[kv])
        def _():
            for i in (0, 1):
                leg2(i, kv).wait_send()

        hop(own, s1, s1_sem, kv, sibling).wait_send()
        hop(a1, s2, s2_sem, kv, sibling).wait_send()


def local(queries, cache_keys, cache_values, stretch_keys, stretch_values, verticals, slashes):
    smem = pl.BlockSpec(memory_space=pltpu.SMEM)
    hbm = pl.BlockSpec(memory_space=pl.ANY)
    dma = pltpu.SemaphoreType.DMA
    vmem = pltpu.VMEM
    return pl.pallas_call(
        kernel,
        out_shape=jax.ShapeDtypeStruct((GROUP, QROWS, HD), BF16),
        in_specs=[smem, smem] + [hbm] * 5,
        out_specs=hbm,
        scratch_shapes=[
            vmem((GROUP, QROWS, HD), BF16),
            vmem((2, CB, BLK, HD), BF16),
            vmem((2, 3 * QB, BLK, HD), BF16),
            vmem((2, 3 * QB, BLK, HD), BF16),
            vmem((2, QB, BLK, HD), BF16),
            vmem((2, BLK, HD), BF16),
            vmem((NY, NV * PART, HD), BF16),
            vmem((2, NY, NV * PART, HD), BF16),
            vmem((NY, NV * PART, HD), BF16),
            vmem((NY, FROWS, HD), BF16),
            vmem((3, FROWS, HD), BF16),
            vmem((3, FROWS, HD), BF16),
            vmem((2, NY, FROWS, HD), BF16),
            vmem((2, NY, SROWS, HD), BF16),
            vmem((NY * FROWS, HD), BF16),
            vmem((NY * FROWS, 2 * HD), BF16),
            vmem((NY * SROWS, HD), BF16),
            vmem((NY * SROWS, 2 * HD), BF16),
            vmem((QB, 4 * BLK, HD), BF16),
            vmem((QB, 4 * BLK, 2 * HD), BF16),
            vmem((QB, 2 * BLK, HD), BF16),
            vmem((QB, 2 * BLK, 2 * HD), BF16),
            vmem((GROUP, QROWS, 2 * HD), F32),
            vmem((GROUP, QROWS, HD), F32),
            vmem((GROUP, QROWS, HD), BF16),
            dma((5,)),
            dma((QB,)),
            dma((2,)),
            dma((6,)),
            dma((4,)),
            dma((4,)),
            dma((6,)),
            dma((2 * NY,)),
            dma((4,)),
            dma((NZ,)),
            dma((NZ,)),
            dma((6,)),
            dma((2 * NY,)),
            dma((4,)),
            dma((4,)),
            dma((4,)),
            dma((4,)),
            dma((4,)),
        ],
        compiler_params=pltpu.CompilerParams(collective_id=0, has_side_effects=True, vmem_limit_bytes=60 * 2**20),
        cost_estimate=pl.CostEstimate(flops=3500000000, bytes_accessed=4000000, transcendentals=7000000),
        name="sparse_attention",
    )(
        verticals,
        slashes,
        queries,
        cache_keys.reshape(CB, BLK, HD),
        cache_values.reshape(CB, BLK, HD),
        stretch_keys.reshape(QB, BLK, HD),
        stretch_values.reshape(QB, BLK, HD),
    )


def solution(mesh):
    return jax.shard_map(
        local,
        mesh=mesh,
        in_specs=(
            P("head", "ctx", None),
            P("head", "ctx", None),
            P("head", "ctx", None),
            P("head", "ctx", None),
            P("head", "ctx", None),
            P("head", None),
            P("head", None),
        ),
        out_specs=P("head", "ctx", None),
        check_vma=False,
    )
```

```python
import math

import jax
import jax.numpy as jnp
from jax import lax
from jax.experimental import pallas as pl
from jax.experimental.pallas import tpu as pltpu
from jax.sharding import PartitionSpec as P

BLK = 128
HD = 128
NV = 8
SPAN = 4
GROUP = 4
NY, NZ = 4, 8
LAST = 2 * NY * NZ
QROWS = 1024
QB = QROWS // BLK
CROWS = 2048
CB = CROWS // BLK
LASTBLOCK = LAST * CB - 1
PART = BLK // NY
FREE = 5
FIXED = NV - FREE
FROWS = FREE * PART
SROWS = FIXED * PART
MESH = pl.DeviceIdType.MESH
COEF = math.log2(math.e) / math.sqrt(HD)
F32 = jnp.float32
BF16 = jnp.bfloat16


def tile(q, k, v, m, acc, keep=None):
    scores = lax.dot_general(q, k, (((1,), (1,)), ((), ())), preferred_element_type=F32)
    if keep is not None:
        scores = jnp.where(keep, scores, -jnp.inf)
    top = jnp.max(scores, axis=1, keepdims=True)
    new = top if m is None else jnp.maximum(m, top)
    p = jnp.exp2((scores - new) * COEF).astype(BF16)
    o = jnp.dot(p, v, preferred_element_type=F32)
    if m is not None:
        o = acc * jnp.exp2((m - new) * COEF) + o
    return new, o


def one_if(lo, hi, x):
    return jnp.minimum(jnp.maximum(x - (lo - 1), 0), 1) * jnp.minimum(jnp.maximum(hi + 1 - x, 0), 1)


def sort_listed(verts):
    listed = [verts[0, j] for j in range(NV)]
    free = [one_if(CB, LASTBLOCK - 1, v) for v in listed]
    at = [0] * FREE
    count = 0
    for v, is_free in zip(listed, free):
        for t in range(FREE):
            at[t] = at[t] + v * is_free * one_if(t, t, count)
        count = count + is_free
    low = 0
    for v in listed:
        low = low + v * one_if(1, CB - 1, v)
    return at, low


def kernel(
    verts, slashes, q_hbm, ck_hbm, cv_hbm, sk_hbm, sv_hbm, out_hbm,
    q_v, cache, near, older, stop, gate, offer, pair, mixed, yb, zb1, zb2, far, fixed,
    far_k, far_v, fix_k, fix_v, near_k, near_v, old_k, old_v, acc_s, max_s, out_v,
    in_sem, out_sem, pair_sem, y_sem, z1_sem, z2_sem, ag_sem, fs_sem,
    fy_sem, fz0_sem, fz7_sem, fg_sem, ff_sem, a1_sem, a2_sem, s1_sem, s2_sem, stop_sem,
):
    me = lax.axis_index("ctx")
    c = lax.rem(me, 2)
    z = lax.rem(lax.div(me, 2), NZ)
    y = lax.div(me, 2 * NZ)

    def at(yy, zz, cc):
        return {"ctx": (yy * NZ + zz) * 2 + cc}

    sibling = at(y, z, 1 - c)
    y_peer = [at(lax.rem(y + k, NY), z, c) for k in range(1, NY)]
    z_peer = [at(y, lax.rem(z + k, NZ), c) for k in range(NZ)]
    ahead = {"ctx": lax.rem(me + 2, LAST)}
    behind = {"ctx": lax.rem(me - 2 + LAST, LAST)}
    a1, s1, own = (near.at[:, i * QB : (i + 1) * QB] for i in range(3))
    a2, s2 = (older.at[:, i * QB : (i + 1) * QB] for i in range(2))
    sends = me + 2 < LAST
    gets1 = me >= 2
    gets2 = me >= 4
    first_z = z == 0
    last_z = z == NZ - 1

    loads = [
        pltpu.make_async_copy(ck_hbm, cache.at[0], in_sem.at[0]),
        pltpu.make_async_copy(cv_hbm, cache.at[1], in_sem.at[1]),
        pltpu.make_async_copy(sk_hbm, own.at[0], in_sem.at[2]),
        pltpu.make_async_copy(sv_hbm, own.at[1], in_sem.at[3]),
        pltpu.make_async_copy(q_hbm, q_v, in_sem.at[4]),
    ]
    for load in loads:
        load.start()

    barrier = pltpu.get_barrier_semaphore()
    peers = [sibling] + y_peer + z_peer[1:] + [ahead, behind]
    for peer in peers:
        pl.semaphore_signal(barrier, inc=1, device_id=peer, device_id_type=MESH)

    free, low = sort_listed(verts)
    offered = [lax.rem(v, CB) for v in free] + [0, low, CB - 1]

    def part(j):
        return slice(j * PART, (j + 1) * PART)

    loads[0].wait()
    loads[1].wait()
    for j, block in enumerate(offered):
        pair[pl.ds(c, 1), :, part(j), :] = cache[pl.ds(c, 1), pl.ds(block, 1)].reshape(1, NY, PART, HD)
        offer[:, part(j), :] = cache[pl.ds(1 - c, 1), pl.ds(block, 1)].reshape(NY, PART, HD)
    pl.semaphore_wait(barrier, len(peers))

    def remote(src, dst, send_sem, recv_sem, to):
        return pltpu.make_async_remote_copy(
            src_ref=src, dst_ref=dst, send_sem=send_sem, recv_sem=recv_sem, device_id=to, device_id_type=MESH
        )

    pair_out = remote(offer, pair.at[c], pair_sem.at[0], pair_sem.at[1], sibling)
    pair_out.start()
    loads[2].wait()
    loads[3].wait()

    def hop(src, dst, sem, kv, to):
        return remote(src.at[kv], dst.at[kv], sem.at[kv], sem.at[2 + kv], to)

    in_row = z < NZ - 1
    leaves_row = jnp.logical_and(last_z, sends)
    passes_keys = jnp.logical_and(first_z, y < NY - 1)
    passes_values = jnp.logical_and(last_z, y > 0)
    corner = (z_peer[1], y_peer[0])

    def leg1(i, kv):
        return remote((own, a1)[i].at[kv], stop.at[i], (a1_sem, a2_sem)[i].at[kv], stop_sem.at[i], corner[kv])

    def leg2(i, kv):
        sem = (a1_sem, a2_sem)[i].at[2 + kv]
        return remote(stop.at[i], (a1, a2)[i].at[kv], stop_sem.at[2 + i], sem, corner[1 - kv])

    def stretch_step(step):
        for kv in (0, 1):
            if step == 0:

                @pl.when(jnp.logical_and(sends, in_row))
                def _():
                    hop(own, a1, a1_sem, kv, ahead).start()

            if step == 0:

                @pl.when(leaves_row)
                def _():
                    leg1(0, kv).start()

            if step == (1, 2)[kv]:

                @pl.when((passes_keys, passes_values)[kv])
                def _():
                    leg1(0, kv).wait_recv()
                    leg2(0, kv).start()

            if step == 4:

                @pl.when(gets1)
                def _():
                    hop(own, a1, a1_sem, kv, behind).wait_recv()

                @pl.when(c == 0)
                def _():
                    hop(a1, s2, s2_sem, kv, sibling).start()

                @pl.when(c == 1)
                def _():
                    hop(a1, s1, s1_sem, kv, sibling).start()

                @pl.when(jnp.logical_and(gets1, in_row))
                def _():
                    hop(a1, a2, a2_sem, kv, ahead).start()

                @pl.when(leaves_row)
                def _():
                    leg1(1, kv).start()

            if step == 5:

                @pl.when((passes_keys, passes_values)[kv])
                def _():
                    leg1(1, kv).wait_recv()
                    leg2(1, kv).start()

    stretch_step(0)

    @pl.when(jnp.logical_not(gets1))
    def _():
        near[:, :QB] = jnp.zeros((2, QB, BLK, HD), BF16)

    @pl.when(jnp.logical_not(gets2))
    def _():
        older[:, :QB] = jnp.zeros((2, QB, BLK, HD), BF16)

    gate[0] = jnp.zeros((BLK, HD), BF16)
    gate[1] = jnp.ones((BLK, HD), BF16)
    far_v[:, HD:] = jnp.ones((NY * FROWS, HD), BF16)
    fix_v[:, HD:] = jnp.ones((NY * SROWS, HD), BF16)

    owner = [lax.div(v, CB) for v in free]
    owner_y = [lax.div(d, 2 * NZ) for d in owner]
    owner_z = [lax.rem(lax.div(d, 2), NZ) for d in owner]
    owner_c = [lax.rem(d, 2) for d in owner]

    remote(offer, pair.at[1 - c], pair_sem.at[0], pair_sem.at[1], sibling).wait_recv()
    for j in range(FREE):
        mixed[:, part(j), :] = pair[pl.ds(owner_c[j], 1), :, part(j), :][0]
    y_out = []
    for k in range(1, NY):
        to = lax.rem(y + k, NY)
        y_out.append(
            remote(mixed.at[to, :FROWS], yb.at[y], y_sem.at[k - 1], y_sem.at[2 + k], y_peer[k - 1])
        )
        y_out[-1].start()
    yb[pl.ds(y, 1)] = mixed[pl.ds(y, 1), :FROWS, :]
    mixed[:, FROWS : FROWS + 2 * PART, :] = pair[0, :, FROWS : FROWS + 2 * PART, :]
    mixed[:, FROWS + 2 * PART :, :] = pair[1, :, FROWS + 2 * PART :, :]

    @pl.when(c == 0)
    def _():
        for kv in (0, 1):
            hop(own, s1, s1_sem, kv, sibling).start()

    halves = (
        (jnp.logical_and(first_z, y == 0), first_z, 0, 2 * PART, fz0_sem),
        (jnp.logical_and(last_z, y == NY - 1), last_z, 2 * PART, SROWS, fz7_sem),
    )

    def fixed_y(k, lo, hi):
        to = lax.rem(y + k, NY)
        return remote(
            mixed.at[to, FROWS + lo : FROWS + hi], fixed.at[c, to, lo:hi], fy_sem.at[k - 1], fy_sem.at[3], y_peer[k - 1]
        )

    def fixed_z(k, lo, hi, sem):
        return remote(fixed.at[c, y, lo:hi], fixed.at[c, y, lo:hi], sem.at[k], sem.at[0], z_peer[k])

    for root, line, lo, hi, sem in halves:

        @pl.when(root)
        def _():
            for k in range(1, NY):
                fixed_y(k, lo, hi).start()
            fixed[pl.ds(c, 1), pl.ds(y, 1), lo:hi, :] = mixed[pl.ds(y, 1), FROWS + lo : FROWS + hi, :][None]

    for k in range(1, NY):
        frm = lax.rem(y + NY - k, NY)
        remote(mixed.at[frm, :FROWS], yb.at[frm], y_sem.at[k - 1], y_sem.at[2 + k], y_peer[k - 1]).wait_recv()
    stretch_step(1)
    for j in range(FREE):
        zb1[1, part(j), :] = yb[pl.ds(owner_y[j], 1), part(j), :][0]
    z1_out = [
        remote(zb1.at[1], zb1.at[0], z1_sem.at[0], z1_sem.at[2], z_peer[1]),
        remote(zb1.at[1], zb1.at[2], z1_sem.at[1], z1_sem.at[3], z_peer[NZ - 1]),
    ]
    for copy in z1_out:
        copy.start()

    for root, line, lo, hi, sem in halves:

        @pl.when(jnp.logical_and(line, jnp.logical_not(root)))
        def _():
            fixed_y(1, lo, hi).wait_recv()

        @pl.when(line)
        def _():
            for k in range(1, NZ):
                fixed_z(k, lo, hi, sem).start()

    for copy in z1_out:
        copy.wait_recv()
    stretch_step(2)
    off = [lax.rem(o - z + NZ, NZ) for o in owner_z]
    for j in range(FREE):
        slot = 1 + one_if(1, 1, off[j]) - one_if(NZ - 1, NZ - 1, off[j])
        zb2[1, part(j), :] = zb1[pl.ds(slot, 1), part(j), :][0]
    z2_out = [
        remote(zb2.at[1], zb2.at[0], z2_sem.at[0], z2_sem.at[2], z_peer[3]),
        remote(zb2.at[1], zb2.at[2], z2_sem.at[1], z2_sem.at[3], z_peer[NZ - 3]),
    ]
    for copy in z2_out:
        copy.start()

    for root, line, lo, hi, sem in halves:

        @pl.when(jnp.logical_not(line))
        def _():
            fixed_z(1, lo, hi, sem).wait_recv()

    def gather(buf, sem, k):
        return remote(buf.at[c, y], buf.at[c, y], sem.at[k - 1], sem.at[2 + k], y_peer[k - 1])

    def gathered(buf, sem, k):
        frm = lax.rem(y + NY - k, NY)
        return remote(buf.at[c, frm], buf.at[c, frm], sem.at[k - 1], sem.at[2 + k], y_peer[k - 1])

    def share(buf, sem, k):
        frm = lax.rem(y + NY - k, NY)
        return remote(buf.at[c, frm], buf.at[c, frm], sem.at[k], sem.at[NY + k], sibling)

    def shared(buf, sem, k):
        frm = lax.rem(y + NY - k, NY)
        return remote(buf.at[1 - c, frm], buf.at[1 - c, frm], sem.at[k], sem.at[NY + k], sibling)

    for k in range(1, NY):
        gather(fixed, fg_sem, k).start()
    share(fixed, ff_sem, 0).start()

    for k in range(1, NY):
        gathered(fixed, fg_sem, k).wait_recv()
        share(fixed, ff_sem, k).start()

    for copy in z2_out:
        copy.wait_recv()
    for j in range(FREE):
        slot = 1 + one_if(2, 4, off[j]) - one_if(5, 6, off[j])
        far[pl.ds(c, 1), pl.ds(y, 1), part(j), :] = zb2[pl.ds(slot, 1), part(j), :][None]
    for k in range(1, NY):
        gather(far, ag_sem, k).start()
    share(far, fs_sem, 0).start()

    stretch_step(4)

    loads[4].wait()
    for kv in (0, 1):
        hop(own, s1, s1_sem, kv, sibling).wait_recv()
    for k in range(NY):
        shared(fixed, ff_sem, k).wait_recv()
    fix_k[...] = fixed[0].reshape(NY * SROWS, HD)
    fix_v[:, :HD] = fixed[1].reshape(NY * SROWS, HD)
    older[:, 2 * QB :] = near[:, :QB]

    def diagonal(b, i, ring, offset, k_ref, v_ref, rows):
        s = slashes[0, i]
        counts = jnp.minimum(jnp.maximum(me * QB + b - s + 1, 0), 1)
        yes = gate[pl.ds(counts, 1)][0]
        no = gate[pl.ds(1 - counts, 1)][0]
        head_row = jnp.broadcast_to(near[0, 2 * QB + b, 0:16, :][0:1], (BLK, HD))
        block = pl.ds(jnp.minimum(jnp.maximum(offset + b - s, 0), 3 * QB - 1), 1)
        k_ref[b, rows, :] = ring[0, block][0] * yes + head_row * no
        v_ref[b, rows, :HD] = ring[1, block][0] * yes
        v_ref[b, rows, HD:] = yes

    def block_rows(b):
        return pl.ds(pl.multiple_of(b * BLK, BLK), BLK)

    def near_block(b, _):
        diagonal(b, 0, near, 2 * QB, near_k, near_v, slice(0, BLK))
        diagonal(b, 1, near, 2 * QB, near_k, near_v, slice(BLK, 2 * BLK))
        near_k[b, 2 * BLK : 3 * BLK, :] = near[0, 2 * QB + b]
        near_v[b, 2 * BLK : 3 * BLK, :HD] = near[1, 2 * QB + b]
        near_v[b, 2 * BLK : 3 * BLK, HD:] = jnp.ones((BLK, HD), BF16)
        near_k[b, 3 * BLK :, :] = fix_k[:BLK, :]
        near_v[b, 3 * BLK :, :] = fix_v[:BLK, :]
        q = q_v[:, block_rows(b), :].reshape(GROUP * BLK, HD)
        t = lax.rem(lax.broadcasted_iota(jnp.int32, (GROUP * BLK, 2 * BLK), 0), BLK)
        u = lax.broadcasted_iota(jnp.int32, (GROUP * BLK, 2 * BLK), 1)
        keep = jnp.logical_or(u <= t, u >= BLK)
        m, acc = tile(q, near_k[b, 2 * BLK :, :], near_v[b, 2 * BLK :, :], None, None, keep)
        m, acc = tile(q, near_k[b, : 2 * BLK, :], near_v[b, : 2 * BLK, :], m, acc)
        m, acc = tile(q, fix_k[BLK:, :], fix_v[BLK:, :], m, acc)
        acc_s[:, block_rows(b), :] = acc.reshape(GROUP, BLK, 2 * HD)
        max_s[:, block_rows(b), :] = jnp.broadcast_to(m, (GROUP * BLK, HD)).reshape(GROUP, BLK, HD)
        return 0

    lax.fori_loop(0, QB, near_block, 0, unroll=True)

    for k in range(1, NY):
        gathered(far, ag_sem, k).wait_recv()
        share(far, fs_sem, k).start()
    stretch_step(5)
    for k in range(NY):
        shared(far, fs_sem, k).wait_recv()

    def receive_relayed(where):
        for kv in (0, 1):

            @pl.when(jnp.logical_and(gets2, where))
            def _():
                hop(a1, a2, a2_sem, kv, behind).wait_recv()

            @pl.when(jnp.logical_and(c == 1, where))
            def _():
                hop(a2, s2, s2_sem, kv, sibling).start()

    receive_relayed(z > 0)
    far_k[...] = far[0].reshape(NY * FROWS, HD)
    far_v[:, :HD] = far[1].reshape(NY * FROWS, HD)

    def far_head(h, _):
        q = q_v[h]
        m, acc = jnp.max(max_s[h], axis=1, keepdims=True), acc_s[h]
        for lo in range(0, NY * FROWS, 2 * BLK):
            hi = min(lo + 2 * BLK, NY * FROWS)
            m, acc = tile(q, far_k[lo:hi, :], far_v[lo:hi, :], m, acc)
        acc_s[h] = acc
        max_s[h] = jnp.broadcast_to(m, (QROWS, HD))
        return 0

    lax.fori_loop(0, GROUP, far_head, 0, unroll=True)

    receive_relayed(first_z)
    for kv in (0, 1):
        hop(a1, s2, s2_sem, kv, sibling).wait_recv()

    def old_block(b, _):
        diagonal(b, 2, older, SPAN * QB, old_k, old_v, slice(0, BLK))
        diagonal(b, 3, older, SPAN * QB, old_k, old_v, slice(BLK, 2 * BLK))
        rows = block_rows(b)
        q = q_v[:, rows, :].reshape(GROUP * BLK, HD)
        m = jnp.max(max_s[:, rows, :].reshape(GROUP * BLK, HD), axis=1, keepdims=True)
        m, acc = tile(q, old_k[b], old_v[b], m, acc_s[:, rows, :].reshape(GROUP * BLK, 2 * HD))
        out_v[:, rows, :] = (acc[:, :HD] / acc[:, HD:]).astype(BF16).reshape(GROUP, BLK, HD)
        pltpu.make_async_copy(out_v.at[:, rows], out_hbm.at[:, rows], out_sem.at[b]).start()
        return 0

    lax.fori_loop(0, QB, old_block, 0, unroll=True)

    for b in range(QB):
        rows = pl.ds(b * BLK, BLK)
        pltpu.make_async_copy(out_v.at[:, rows], out_hbm.at[:, rows], out_sem.at[b]).wait()
    for copy in [pair_out] + y_out + z1_out + z2_out:
        copy.wait_send()
    for k in range(1, NY):
        gather(fixed, fg_sem, k).wait_send()
        gather(far, ag_sem, k).wait_send()
    for k in range(NY):
        share(fixed, ff_sem, k).wait_send()
        share(far, fs_sem, k).wait_send()
    for root, line, lo, hi, sem in halves:

        @pl.when(root)
        def _():
            for k in range(1, NY):
                fixed_y(k, lo, hi).wait_send()

        @pl.when(line)
        def _():
            for k in range(1, NZ):
                fixed_z(k, lo, hi, sem).wait_send()

    for kv in (0, 1):

        @pl.when(sends)
        def _():
            hop(own, a1, a1_sem, kv, ahead).wait_send()

        @pl.when(jnp.logical_and(gets1, sends))
        def _():
            hop(a1, a2, a2_sem, kv, ahead).wait_send()

        @pl.when((passes_keys, passes_values)[kv])
        def _():
            for i in (0, 1):
                leg2(i, kv).wait_send()

        hop(own, s1, s1_sem, kv, sibling).wait_send()
        hop(a1, s2, s2_sem, kv, sibling).wait_send()


def local(queries, cache_keys, cache_values, stretch_keys, stretch_values, verticals, slashes):
    smem = pl.BlockSpec(memory_space=pltpu.SMEM)
    hbm = pl.BlockSpec(memory_space=pl.ANY)
    dma = pltpu.SemaphoreType.DMA
    vmem = pltpu.VMEM
    return pl.pallas_call(
        kernel,
        out_shape=jax.ShapeDtypeStruct((GROUP, QROWS, HD), BF16),
        in_specs=[smem, smem] + [hbm] * 5,
        out_specs=pl.BlockSpec(memory_space=pltpu.HBM),
        scratch_shapes=[
            vmem((GROUP, QROWS, HD), BF16),
            vmem((2, CB, BLK, HD), BF16),
            vmem((2, 3 * QB, BLK, HD), BF16),
            vmem((2, 3 * QB, BLK, HD), BF16),
            vmem((2, QB, BLK, HD), BF16),
            vmem((2, BLK, HD), BF16),
            vmem((NY, NV * PART, HD), BF16),
            vmem((2, NY, NV * PART, HD), BF16),
            vmem((NY, NV * PART, HD), BF16),
            vmem((NY, FROWS, HD), BF16),
            vmem((3, FROWS, HD), BF16),
            vmem((3, FROWS, HD), BF16),
            vmem((2, NY, FROWS, HD), BF16),
            vmem((2, NY, SROWS, HD), BF16),
            vmem((NY * FROWS, HD), BF16),
            vmem((NY * FROWS, 2 * HD), BF16),
            vmem((NY * SROWS, HD), BF16),
            vmem((NY * SROWS, 2 * HD), BF16),
            vmem((QB, 4 * BLK, HD), BF16),
            vmem((QB, 4 * BLK, 2 * HD), BF16),
            vmem((QB, 2 * BLK, HD), BF16),
            vmem((QB, 2 * BLK, 2 * HD), BF16),
            vmem((GROUP, QROWS, 2 * HD), F32),
            vmem((GROUP, QROWS, HD), F32),
            vmem((GROUP, QROWS, HD), BF16),
            dma((5,)),
            dma((QB,)),
            dma((2,)),
            dma((6,)),
            dma((4,)),
            dma((4,)),
            dma((6,)),
            dma((2 * NY,)),
            dma((4,)),
            dma((NZ,)),
            dma((NZ,)),
            dma((6,)),
            dma((2 * NY,)),
            dma((4,)),
            dma((4,)),
            dma((4,)),
            dma((4,)),
            dma((4,)),
        ],
        compiler_params=pltpu.CompilerParams(collective_id=0, has_side_effects=True, vmem_limit_bytes=60 * 2**20),
        cost_estimate=pl.CostEstimate(flops=3500000000, bytes_accessed=4000000, transcendentals=7000000),
        name="sparse_attention",
    )(
        verticals,
        slashes,
        queries,
        cache_keys.reshape(CB, BLK, HD),
        cache_values.reshape(CB, BLK, HD),
        stretch_keys.reshape(QB, BLK, HD),
        stretch_values.reshape(QB, BLK, HD),
    )


def solution(mesh):
    return jax.shard_map(
        local,
        mesh=mesh,
        in_specs=(
            P("head", "ctx", None),
            P("head", "ctx", None),
            P("head", "ctx", None),
            P("head", "ctx", None),
            P("head", "ctx", None),
            P("head", None),
            P("head", None),
        ),
        out_specs=P("head", "ctx", None),
        check_vma=False,
    )
```
